512 devices in a mesh: dp: 64 (over y_lo, z, x), tensor: 8 (over y_hi, core).
Axes of the slice: x: 4, y: 8 (y_hi: 4, y_lo: 2; y = y_hi * 2 + y_lo), z: 8, core: 2. Of those that a mesh axis runs over, the one named last changes fastest.
Arguments:
- activations: bfloat16 [65536, 3072], P(('dp', 'tensor'))
- norm_gain: bfloat16 [3072], replicated, may hold values from 0.099609375 to 1.8984375
- query_weight: bfloat16 [3072, 3072], P('dp', 'tensor')
- key_weight: bfloat16 [3072, 512], P('dp')
- value_matrix: bfloat16 [3072, 512], P('dp'), may hold values from -0.109375 to 0.109375
- output_weight: bfloat16 [3072, 3072], P('dp', 'tensor'), may hold values from -0.109375 to 0.109375
- document_lengths: int32 [64, 3], replicated, may hold values from 1 to 3, 8 in all within a row
- doc_dest: int32 [64, 3], replicated, may hold values from 0 to 63, as said below
Outputs:
- attended: bfloat16 [131072, 3072], P('dp', 'tensor')
The draws below stay inside these ranges and needn't reach their ends.
Inputs may be any that keep to these rules, and one draw needn't show every extreme that they name: `document_lengths`: each row sums to 8; its largest entry is exactly 3. doc_dest[s, j] is either s or the next shard s + 1, the last shard wrapping to shard 0.
All inputs are finite; a program needn't handle non-finite values.
Results may differ from the reference program's by a relative error of at most 0.012.
The reference program's roundings to bfloat16 on the way count: a program that leaves them out, or rounds other values in their place, can miss the bound.
Values may be sent and summed in bfloat16 or wider, within the bound.
No kernel may reach another device: no remote copies, remote signals or barrier semaphores. Data moves between devices by JAX's collectives and lax.ppermute only.
A program may use at most 64 MiB of HBM per device.

```python
import math
import jax
import jax.numpy as jnp
import numpy as np
from jax import lax

MODEL_WIDTH = 3072
QUERY_HEADS = 24
KEY_VALUE_HEADS = 4
HEAD_SIZE = 128
BLK = 128
BLK_DEV = 8
DOCS = 3
LMAX = 3
SHARD_TOKENS = 1024
TOKENS = 65536
N_DP = 64


def shared_columns(key):
    return jax.random.normal(jax.random.fold_in(key, 101), (MODEL_WIDTH, 2 * HEAD_SIZE), jnp.float32)


def draw_activations(key, part):
    key = jax.random.fold_in(key, 11)
    base_key, row_key, col_key = jax.random.split(key, 3)
    row_scale = 10.0 ** jax.random.uniform(row_key, (TOKENS, 1), jnp.float32)
    col_scale = 10.0 ** jax.random.uniform(col_key, (1, MODEL_WIDTH), jnp.float32)
    values = jax.random.normal(base_key, (TOKENS, MODEL_WIDTH), jnp.float32)
    return (values * row_scale * col_scale * 0.3).astype(jnp.bfloat16)


def draw_query_weight(key, part):
    shared = shared_columns(key)
    key = jax.random.fold_in(key, 12)
    group_width = QUERY_HEADS // KEY_VALUE_HEADS
    local_portion = jax.random.normal(key, (MODEL_WIDTH, QUERY_HEADS * HEAD_SIZE), jnp.float32)
    local_portion = local_portion.at[:, 0:HEAD_SIZE].set(shared[:, 0:HEAD_SIZE])
    local_portion = local_portion.at[:, group_width * HEAD_SIZE:(group_width + 1) * HEAD_SIZE].set(shared[:, HEAD_SIZE:2 * HEAD_SIZE])
    return (local_portion / math.sqrt(MODEL_WIDTH)).astype(jnp.bfloat16)


def draw_key_weight(key, part):
    key = jax.random.fold_in(key, 13)
    local_portion = jax.random.normal(key, (MODEL_WIDTH, KEY_VALUE_HEADS * HEAD_SIZE), jnp.float32)
    return (local_portion / math.sqrt(MODEL_WIDTH)).astype(jnp.bfloat16)


def draw_doc_dest(key, part):
    key = jax.random.fold_in(key, 14)
    hop_count = jax.random.randint(key, (N_DP, DOCS), 0, 2, jnp.int32)
    shard_ids = lax.broadcasted_iota(jnp.int32, (N_DP, DOCS), 0)
    return ((shard_ids + hop_count) % N_DP).astype(jnp.int32)


def block_scale(key, extent, shards, least, top_value):
    factor_of = 1.0
    for axis_at, shards_of in shards:
        steps = jax.random.uniform(jax.random.fold_in(jax.random.fold_in(key, 6), axis_at), (shards_of,), jnp.float32, least / len(shards), top_value / len(shards))
        factor_of = factor_of * jnp.repeat(jnp.exp(steps), extent[axis_at] // shards_of).reshape((-1,) + (1,) * (len(extent) - 1 - axis_at))
    return factor_of


def profile(number_of, total, reach, lean):
    portions = [(1 << 20) // math.isqrt(standing ** lean) + 1 for standing in range(2, number_of + 1)]
    surplus, holding = total - reach - (number_of - 1), [1] * (number_of - 1)
    while surplus > 0:
        movable = [i for i in range(number_of - 1) if holding[i] < reach]
        whole, remaining = sum([portions[i] for i in movable]), surplus
        for i in movable:
            addition = min(reach - holding[i], max(1, remaining * portions[i] // whole), surplus)
            holding[i] = holding[i] + addition
            surplus = surplus - addition
    return np.array([reach] + holding)


def ragged(stream_key, amount, total, bound, slope):
    if amount == 2:
        one = jax.random.randint(stream_key, (), max(1, total - bound), min(bound, total - 1) + 1)
        return jnp.stack([one, total - one])
    lengths = jnp.asarray(profile(amount, total, bound, slope), jnp.int32)
    pairs = (amount - 1) // 2
    source_of, taker = lengths[1:1 + 2 * pairs:2], lengths[2:2 + 2 * pairs:2]
    slack = jnp.minimum(source_of - 1, bound - taker)
    shifted = jax.random.randint(jax.random.fold_in(stream_key, 1), (pairs,), 0, 1 << 20) % (slack + 1)
    lengths = lengths.at[1:1 + 2 * pairs:2].set(source_of - shifted).at[2:2 + 2 * pairs:2].set(taker + shifted)
    return lengths[jax.random.permutation(jax.random.fold_in(stream_key, 2), amount)]


def gaussian(own_key, dims, scale, bound, cuts=(), held_as=jnp.bfloat16):
    loudness = block_scale(own_key, dims, cuts, -0.22, 0.18) if cuts else 1.0
    drawn = jax.random.normal(own_key, dims, jnp.float32) * scale * loudness
    return jnp.minimum(jnp.maximum(drawn, -bound), bound).astype(held_as)


def setup_inputs(seed: int = 0) -> dict:
    seeds = jax.random.split(jax.random.key(seed), 9)
    activations = draw_activations(jax.random.fold_in(seeds[8], 71), 0)
    norm_gain = jnp.clip(1.0 + 0.18 * jax.random.normal(seeds[1], (MODEL_WIDTH,), jnp.float32), 0.099609375, 1.8984375).astype(jnp.bfloat16)
    query_weight = draw_query_weight(jax.random.fold_in(seeds[8], 71), 0)
    key_weight = draw_key_weight(jax.random.fold_in(seeds[8], 71), 0)
    value_matrix = gaussian(seeds[4], (MODEL_WIDTH, KEY_VALUE_HEADS * HEAD_SIZE), MODEL_WIDTH ** -0.5, 0.109375, ((0, 64),))
    output_weight = gaussian(seeds[5], (QUERY_HEADS * HEAD_SIZE, MODEL_WIDTH), (QUERY_HEADS * HEAD_SIZE) ** -0.5, 0.109375, ((0, 64), (1, 8)))
    document_lengths = jax.vmap(lambda own: ragged(own, DOCS, BLK_DEV, LMAX, 0))(jax.random.split(seeds[6], N_DP)).reshape((N_DP, DOCS)).astype(jnp.int32)
    doc_dest = draw_doc_dest(jax.random.fold_in(seeds[8], 71), 0)
    return {"activations": activations, "norm_gain": norm_gain, "query_weight": query_weight, "key_weight": key_weight, "value_matrix": value_matrix, "output_weight": output_weight, "document_lengths": document_lengths, "doc_dest": doc_dest}


EPS = 1e-05

def block_documents(length_row, count_of_rows):
    doc_ends = jnp.cumsum(length_row).astype(jnp.int32) * BLK
    positions = jnp.arange(count_of_rows, dtype=jnp.int32)
    return lax.optimization_barrier(jnp.sum((positions[:, None] >= doc_ends[None, :]).astype(jnp.int32), axis=1)).astype(jnp.int32)

def moved_rows(doc_ids, dest_row, shard_index):
    doc_slots = jnp.arange(dest_row.shape[0], dtype=jnp.int32)
    target = lax.optimization_barrier(jnp.sum(jnp.where(doc_ids[:, None] == doc_slots[None, :], dest_row[None, :], 0), axis=1)).astype(jnp.int32)
    return (target != shard_index).astype(jnp.bfloat16)

def shard_attention(query_rows, rows_of_key, rows_of_value, doc_ids):
    count_of_rows = query_rows.shape[0]
    group_width = QUERY_HEADS // KEY_VALUE_HEADS
    heads_of_query = query_rows.astype(jnp.float32).reshape(count_of_rows, KEY_VALUE_HEADS, group_width, HEAD_SIZE)
    heads_of_key = rows_of_key.astype(jnp.float32).reshape(count_of_rows, KEY_VALUE_HEADS, HEAD_SIZE)
    heads_of_value = rows_of_value.astype(jnp.float32).reshape(count_of_rows, KEY_VALUE_HEADS, HEAD_SIZE)
    positions = jnp.arange(count_of_rows, dtype=jnp.int32)
    allowed = (doc_ids[:, None] == doc_ids[None, :]) & (positions[None, :] <= positions[:, None])
    scores = jnp.einsum('qkgd,skd->kgqs', heads_of_query, heads_of_key) / math.sqrt(HEAD_SIZE)
    scores = jnp.where(allowed[None, None], scores, -jnp.inf)
    row_max = lax.optimization_barrier(jnp.max(scores, axis=-1, keepdims=True))
    exponent = jnp.exp(scores - row_max)
    row_total = lax.optimization_barrier(jnp.sum(exponent, axis=-1))
    rounded = lax.optimization_barrier(exponent.astype(jnp.bfloat16)).astype(jnp.float32)
    mixed_values = jnp.einsum('kgqs,skd->qkgd', rounded, heads_of_value)
    outputs = mixed_values / jnp.transpose(row_total, (2, 0, 1))[..., None]
    return outputs.reshape(count_of_rows, QUERY_HEADS * HEAD_SIZE).astype(jnp.bfloat16)

def reference(activations, norm_gain, query_weight, key_weight, value_matrix, output_weight, document_lengths, doc_dest):
    inputs = activations.astype(jnp.float32)
    mean_square = lax.optimization_barrier(jnp.mean(inputs * inputs, axis=1, keepdims=True))
    normed = (inputs * lax.rsqrt(mean_square + EPS) * norm_gain.astype(jnp.float32)).astype(jnp.bfloat16)
    query_rows = jnp.dot(normed, query_weight, preferred_element_type=jnp.float32).astype(jnp.bfloat16)
    rows_of_key = jnp.dot(normed, key_weight, preferred_element_type=jnp.float32).astype(jnp.bfloat16)
    rows_of_value = jnp.dot(normed, value_matrix, preferred_element_type=jnp.float32).astype(jnp.bfloat16)

    def shard_portion(shard_items):
        shard_queries, shard_keys, shard_values, length_row = shard_items
        doc_ids = block_documents(length_row, SHARD_TOKENS)
        return shard_attention(shard_queries, shard_keys, shard_values, doc_ids)
    attention_layer = lax.map(shard_portion, (query_rows.reshape(N_DP, SHARD_TOKENS, QUERY_HEADS * HEAD_SIZE), rows_of_key.reshape(N_DP, SHARD_TOKENS, KEY_VALUE_HEADS * HEAD_SIZE), rows_of_value.reshape(N_DP, SHARD_TOKENS, KEY_VALUE_HEADS * HEAD_SIZE), document_lengths))
    projected = jnp.dot(attention_layer.reshape(TOKENS, QUERY_HEADS * HEAD_SIZE), output_weight, preferred_element_type=jnp.float32).astype(jnp.bfloat16)
    projected = projected.reshape(N_DP, SHARD_TOKENS, MODEL_WIDTH)
    doc_all = jax.vmap(block_documents, in_axes=(0, None))(document_lengths, SHARD_TOKENS)
    shard_ids = jnp.arange(N_DP, dtype=jnp.int32)
    moved = jax.vmap(moved_rows)(doc_all, doc_dest, shard_ids)
    staying = projected * (1 - moved)[..., None]
    leaving = projected * moved[..., None]
    arriving = jnp.roll(leaving, 1, axis=0)
    return jnp.concatenate([staying, arriving], axis=1).reshape(N_DP * 2 * SHARD_TOKENS, MODEL_WIDTH)
```

```python
import math

import jax
import jax.numpy as jnp
import numpy as np
from jax import lax
from jax.experimental import pallas as pl
from jax.experimental.pallas import tpu as pltpu
from jax.sharding import Mesh, PartitionSpec as P

HEAD_SIZE = 128
BLK = 128
EPS = 1e-05
AXES = ("yl", "z", "x", "yh", "c")
SIZES = (2, 8, 4, 4, 2)
EXTENT = dict(zip(AXES, SIZES))
VMEM = 56 * 1024 * 1024
HEAD_ORDER = (0, 1, 3, 4, 2, 5)


def shift(value, axis, steps):
    count = EXTENT[axis]
    return lax.ppermute(value, axis, [(i, (i + steps) % count) for i in range(count)])


def scatter_pairs(round_index):
    pairs = []
    for yl in range(2):
        for yh in range(4):
            for c in range(2):
                target = ((yh >> 1) * 4 + ((2 * yl + c) ^ round_index)) * 2 + (yh & 1)
                pairs.append(((yl * 4 + yh) * 2 + c, target))
    return pairs


def collect_pairs(round_index):
    pairs = []
    for yl in range(2):
        for yh in range(4):
            for c in range(2):
                slot = yh ^ round_index
                target = ((slot >> 1) * 4 + 2 * yl + c) * 2 + (slot & 1)
                pairs.append(((yl * 4 + yh) * 2 + c, target))
    return pairs


def ring_x(block):
    half = block.shape[0] // 2
    below = shift(block, "x", 1)
    above = shift(block, "x", -1)
    far_low = shift(below[:half], "x", 1)
    far_high = shift(above[half:], "x", -1)
    return block, below, above, far_low, far_high


def copies_of_ring(refs, target, columns, x):
    own, below, above, far_low, far_high = refs
    half = own.shape[0] // 2
    full = own.shape[0]
    pairs = []
    for ref, start, size, offset in (
        (own, 0, full, 0),
        (below, 0, full, 3),
        (above, 0, full, 1),
        (far_low, 0, half, 2),
        (far_high, half, full - half, 2),
    ):
        for yl in range(2):
            pairs.append(
                (ref.at[:, yl], target.at[yl, pl.ds(start, size), (x + offset) & 3, :, columns])
            )
    return pairs


def start_all(pairs, sems, first):
    made = []
    for i, (source, target) in enumerate(pairs):
        copy = pltpu.make_async_copy(source, target, sems.at[first + i])
        copy.start()
        made.append(copy)
    return made


def rows_pairs(pieces, target, yl, c):
    pairs = []
    for i, piece in enumerate(pieces):
        place = 2 * (yl ^ (i >> 1)) + (c ^ (i & 1))
        pairs.append((piece, target.at[place]))
    return pairs


def key_value_kernel(where, n0, n1, n2, n3, b0, b1, b2, b3, b4, out, rows, weight, sems):
    yl, x, c = where[0], where[2], where[4]
    made = start_all(rows_pairs((n0, n1, n2, n3), rows, yl, c), sems, 0)
    made += start_all(
        copies_of_ring((b0, b1, b2, b3, b4), weight, slice(0, 256), x), sems, 4
    )
    for copy in made:
        copy.wait()
    out[...] = jnp.dot(
        rows[...].reshape(512, 3072),
        weight[...].reshape(3072, 256),
        preferred_element_type=jnp.float32,
    ).astype(jnp.bfloat16)


def attention_kernel(
    where, n0, n1, n2, n3, wide, b0, b1, b2, b3, b4, own_kv, halo_kv, out, rows, weight, query, sems
):
    yl, x, yh, c = where[0], where[2], where[3], where[4]
    made = start_all(rows_pairs((n0, n1, n2, n3), rows, yl, c), sems, 0)
    made += start_all(
        [(wide.at[:, :, i], weight.at[i, :, :, :, 0:512]) for i in range(2)], sems, 4
    )
    made += start_all(
        copies_of_ring((b0, b1, b2, b3, b4), weight, slice(512, 768), x), sems, 6
    )
    for copy in made:
        copy.wait()
    query[...] = jnp.dot(
        rows[...].reshape(512, 3072),
        weight[...].reshape(3072, 768),
        preferred_element_type=jnp.float32,
    ).astype(jnp.bfloat16)
    row = lax.broadcasted_iota(jnp.int32, (BLK, 3 * BLK), 0)
    column = lax.broadcasted_iota(jnp.int32, (BLK, 3 * BLK), 1)
    causal = (column >= 2 * BLK) & (column - 2 * BLK <= row)
    scale = 1.0 / math.sqrt(HEAD_SIZE)
    for shard in range(2):
        first_end = where[5 + 2 * shard]
        second_end = where[6 + 2 * shard]

        def document(block):
            return (block >= first_end).astype(jnp.int32) + (block >= second_end).astype(jnp.int32)

        keys = jnp.concatenate(
            [
                halo_kv[shard * 256 : shard * 256 + 256, 0:128],
                own_kv[shard * 256 : shard * 256 + 256, 0:128],
            ],
            axis=0,
        )
        values = jnp.concatenate(
            [
                halo_kv[shard * 256 : shard * 256 + 256, 128:256],
                own_kv[shard * 256 : shard * 256 + 256, 128:256],
            ],
            axis=0,
        )
        for j in range(2):
            block = 2 * yh + j
            mine = document(block)
            near = ((block >= 1) & (document(block - 1) == mine)).astype(jnp.int32)
            far = ((block >= 2) & (document(block - 2) == mine)).astype(jnp.int32)
            open_before = jnp.where(column < BLK, far, near)
            allowed = causal | ((column < 2 * BLK) & (open_before == 1))
            at = shard * 256 + j * BLK
            stacked = jnp.concatenate(
                [query[at : at + BLK, i * 128 : i * 128 + 128] for i in range(6)], axis=0
            )
            window = keys[j * BLK : j * BLK + 3 * BLK]
            scores = (
                lax.dot_general(
                    stacked, window, (((1,), (1,)), ((), ())), preferred_element_type=jnp.float32
                )
                * scale
            )
            scores = jnp.where(allowed[None], scores.reshape(6, BLK, 3 * BLK), -jnp.inf)
            exponent = jnp.exp(scores - jnp.max(scores, axis=-1, keepdims=True))
            total = jnp.sum(exponent, axis=-1, keepdims=True)
            mixed = jnp.dot(
                exponent.astype(jnp.bfloat16).reshape(6 * BLK, 3 * BLK),
                values[j * BLK : j * BLK + 3 * BLK],
                preferred_element_type=jnp.float32,
            )
            mixed = (mixed / total.reshape(6 * BLK, 1)).astype(jnp.bfloat16)
            for i, head in enumerate(HEAD_ORDER):
                out[at : at + BLK, head * 128 : head * 128 + 128] = mixed[i * BLK : i * BLK + BLK]


def output_kernel(
    where, a0, a1, a2, a3, wide, b0, b1, b2, b3, b4, s0, s1, s2, s3, weight, blocks, sems
):
    yl, x, yh, c = where[0], where[2], where[3], where[4]
    made = start_all(
        [(wide.at[:, :, i], weight.at[i, :, :, :, 0:384]) for i in range(2)], sems, 0
    )
    made += start_all(
        copies_of_ring((b0, b1, b2, b3, b4), weight, slice(384, 768), x), sems, 2
    )
    for copy in made:
        copy.wait()
    total = jnp.zeros((512, 768), jnp.float32)
    for i, piece in enumerate((a0, a1, a2, a3)):
        part = weight[yl ^ (i >> 1), pl.ds(4 * (c ^ (i & 1)), 4)]
        total = total + jnp.dot(
            piece[...], part.reshape(768, 768), preferred_element_type=jnp.float32
        )
    for shard in range(2):
        for half in range(2):
            blocks[2 * shard + half] = total[
                shard * 256 : shard * 256 + 256, half * 384 : half * 384 + 384
            ].astype(jnp.bfloat16)
    for r, out in enumerate((s0, s1, s2, s3)):
        out[...] = blocks[yh ^ r]


SMEM_SPEC = pl.BlockSpec(memory_space=pltpu.SMEM)
ANY_SPEC = pl.BlockSpec(memory_space=pl.ANY)
VMEM_SPEC = pl.BlockSpec(memory_space=pltpu.VMEM)
PARAMS = pltpu.CompilerParams(vmem_limit_bytes=VMEM)


def project_key_value(where, pieces, ring):
    return pl.pallas_call(
        key_value_kernel,
        out_shape=jax.ShapeDtypeStruct((512, 256), jnp.bfloat16),
        in_specs=[SMEM_SPEC] + [ANY_SPEC] * 9,
        out_specs=VMEM_SPEC,
        scratch_shapes=[
            pltpu.VMEM((4, 128, 3072), jnp.bfloat16),
            pltpu.VMEM((2, 8, 4, 48, 256), jnp.bfloat16),
            pltpu.SemaphoreType.DMA((14,)),
        ],
        compiler_params=PARAMS,
        name="key_value",
    )(where, *pieces, *ring)


def attend(where, pieces, wide, ring, own_kv, halo_kv):
    return pl.pallas_call(
        attention_kernel,
        out_shape=jax.ShapeDtypeStruct((512, 768), jnp.bfloat16),
        in_specs=[SMEM_SPEC] + [ANY_SPEC] * 10 + [VMEM_SPEC] * 2,
        out_specs=VMEM_SPEC,
        scratch_shapes=[
            pltpu.VMEM((4, 128, 3072), jnp.bfloat16),
            pltpu.VMEM((2, 8, 4, 48, 768), jnp.bfloat16),
            pltpu.VMEM((512, 768), jnp.bfloat16),
            pltpu.SemaphoreType.DMA((16,)),
        ],
        compiler_params=PARAMS,
        name="attend",
    )(where, *pieces, wide, *ring, own_kv, halo_kv)


def project_output(where, pieces, wide, ring):
    piece = jax.ShapeDtypeStruct((256, 384), jnp.bfloat16)
    return pl.pallas_call(
        output_kernel,
        out_shape=(piece,) * 4,
        in_specs=[SMEM_SPEC] + [VMEM_SPEC] * 4 + [ANY_SPEC] * 6,
        out_specs=(VMEM_SPEC,) * 4,
        scratch_shapes=[
            pltpu.VMEM((2, 8, 4, 48, 768), jnp.bfloat16),
            pltpu.VMEM((4, 256, 384), jnp.bfloat16),
            pltpu.SemaphoreType.DMA((12,)),
        ],
        compiler_params=PARAMS,
        name="project_output",
    )(where, *pieces, wide, *ring)


def exchanged(value):
    other = shift(value, "yl", 1)
    return value, shift(value, "c", 1), other, shift(other, "c", 1)


def shards(
    activations,
    norm_gain,
    query_weight,
    key_weight,
    value_matrix,
    output_weight,
    document_lengths,
    doc_dest,
):
    yl, z, x, yh, c = (lax.axis_index(axis) for axis in AXES)
    shard_index = (yl * 8 + z) * 4 + x
    ends = jnp.cumsum(document_lengths, axis=1)

    def row_of(table, index):
        return lax.dynamic_index_in_dim(table, index, 0, keepdims=False)

    group_ends = [row_of(ends, (i * 8 + z) * 4 + x) for i in range(2)]
    where = jnp.stack(
        [yl, z, x, yh, c]
        + [group_ends[0][0], group_ends[0][1], group_ends[1][0], group_ends[1][1]]
    ).astype(jnp.int32)

    key_or_value = lax.dynamic_slice_in_dim(
        jnp.where(c == 0, key_weight, value_matrix), yh * 128, 128, 1
    )
    packed = jnp.concatenate([key_or_value, query_weight, output_weight], axis=1)
    rounds = jnp.stack(
        [lax.ppermute(packed, ("yl", "yh", "c"), scatter_pairs(r)) for r in range(4)]
    )
    slots = [lax.dynamic_index_in_dim(rounds, s ^ yh, 0, keepdims=False) for s in range(4)]
    low = jnp.stack([slots[0], slots[2]])
    high = jnp.stack([slots[1], slots[3]])
    wide_part = jnp.concatenate(
        [low[..., 128:384], high[..., 128:384], low[..., 512:896]], axis=2
    )
    ring_part = jnp.concatenate(
        [
            low[..., 0:128],
            high[..., 0:128],
            low[..., 384:512],
            high[..., 384:512],
            high[..., 512:896],
        ],
        axis=2,
    )
    wide_x = lax.all_gather(wide_part, "x", axis=0, tiled=False)
    ring_z = lax.all_gather(ring_part, "z", axis=0, tiled=False)
    wide_query = lax.all_gather(wide_x[..., 0:512], "z", axis=0, tiled=False)
    wide_output = lax.all_gather(wide_x[..., 512:896], "z", axis=0, tiled=False)

    inputs = activations.astype(jnp.float32)
    mean_square = jnp.mean(inputs * inputs, axis=1, keepdims=True)
    normed = (inputs * lax.rsqrt(mean_square + EPS) * norm_gain.astype(jnp.float32)).astype(
        jnp.bfloat16
    )
    pieces = exchanged(normed)

    ring_key_value = ring_x(ring_z[..., 0:256])
    own_kv = project_key_value(where, pieces, ring_key_value)
    halo_kv = shift(own_kv, "yh", 1)
    ring_query = ring_x(ring_z[..., 256:512])
    attention = attend(where, pieces, wide_query, ring_query, own_kv, halo_kv)
    ring_output = ring_x(ring_z[..., 512:896])
    gathered = exchanged(attention)
    sent = project_output(where, gathered, wide_output, ring_output)

    taken = [
        lax.ppermute(sent[r], ("yl", "yh", "c"), collect_pairs(r)) for r in range(4)
    ]
    own_slot = 2 * yl + c
    own_ends = row_of(ends, shard_index)
    own_dest = row_of(doc_dest, shard_index)
    blocks = jnp.arange(8, dtype=jnp.int32)
    block_docs = (blocks >= own_ends[0]).astype(jnp.int32) + (blocks >= own_ends[1]).astype(
        jnp.int32
    )
    target = jnp.sum(
        jnp.where(block_docs[:, None] == jnp.arange(3)[None, :], own_dest[None, :], 0), axis=1
    )
    moved = (target != shard_index).astype(jnp.bfloat16)
    leaving = []
    staying = []
    for r in range(4):
        flags = lax.dynamic_slice_in_dim(moved, 2 * (own_slot ^ r), 2, 0)
        flags = jnp.broadcast_to(flags[:, None, None], (2, BLK, 1)).reshape(2 * BLK, 1)
        leaving.append(taken[r] * flags)
        staying.append(taken[r] * (1 - flags))
    count = 64
    pairs = [(i, (i + 1) % count) for i in range(count)]
    arrived = []
    for i in range(2):
        arrived.append(
            lax.ppermute(
                jnp.stack([leaving[2 * i], leaving[2 * i + 1]]), ("yl", "z", "x"), pairs
            )
        )
    arrived = jnp.concatenate(arrived, axis=0)
    kept = jnp.stack(staying)
    before = (shard_index + 63) % 64
    before_slot = 2 * (before // 32) + c
    parts = [lax.dynamic_index_in_dim(kept, q ^ own_slot, 0, keepdims=False) for q in range(4)]
    parts += [
        lax.dynamic_index_in_dim(arrived, q ^ before_slot, 0, keepdims=False) for q in range(4)
    ]
    return jnp.concatenate(parts, axis=0)


def solution(mesh):
    fine = Mesh(np.asarray(mesh.devices).reshape(SIZES), AXES)
    dp, tensor = ("yl", "z", "x"), ("yh", "c")
    in_specs = (
        P(dp + tensor, None),
        P(),
        P(dp, tensor),
        P(dp, None),
        P(dp, None),
        P(dp, tensor),
        P(),
        P(),
    )
    return jax.shard_map(
        shards, mesh=fine, in_specs=in_specs, out_specs=P(dp, tensor), check_vma=False
    )
```

```python
import functools
import math

import jax
import jax.numpy as jnp
import numpy as np
from jax import lax
from jax.experimental import pallas as pl
from jax.experimental.pallas import tpu as pltpu
from jax.sharding import Mesh, PartitionSpec as P

BLK = 128
EPS = 1e-05
SCALE = 1.0 / math.sqrt(128)
AXES = ("yl", "z", "x", "yh", "c")
SIZES = (2, 8, 4, 4, 2)
EXTENT = dict(zip(AXES, SIZES))
HALF = 512
VMEM = 56 * 1024 * 1024
PARAMS = pltpu.CompilerParams(vmem_limit_bytes=VMEM)
SMEM_SPEC = pl.BlockSpec(memory_space=pltpu.SMEM)
ANY_SPEC = pl.BlockSpec(memory_space=pl.ANY)
VMEM_SPEC = pl.BlockSpec(memory_space=pltpu.VMEM)
PLACES = np.stack(
    [(np.arange(512) // 8) % 4, np.arange(512) // 8], axis=1
).astype(np.int32)


def shift(value, axis, steps):
    count = EXTENT[axis]
    return lax.ppermute(value, axis, [(i, (i + steps) % count) for i in range(count)])


def ring_x(block):
    half = block.shape[0] // 2
    below = shift(block, "x", 1)
    above = shift(block, "x", -1)
    return (
        block,
        below,
        above,
        shift(below[:half], "x", 1),
        shift(above[half:], "x", -1),
    )


def ring_pairs(refs, weight, x):
    pairs = []
    for ref, first, offset in zip(refs, (0, 0, 0, 0, 4), (0, 3, 1, 2, 2)):
        for yl in range(2):
            pairs.append(
                (ref.at[:, yl], weight.at[yl, pl.ds(first, ref.shape[0]), (x + offset) & 3])
            )
    return pairs


def start_all(pairs, sems, first):
    made = []
    for i, (source, target) in enumerate(pairs):
        copy = pltpu.make_async_copy(source, target, sems.at[first + i])
        copy.start()
        made.append(copy)
    return made


def document_of(lengths, shard, block):
    first_end = lengths[shard, 0]
    second_end = first_end + lengths[shard, 1]
    return (block >= first_end).astype(jnp.int32) + (block >= second_end).astype(jnp.int32)


def attention_kernel(
    where, lengths, normed, b0, b1, b2, b3, b4, out, rows, weight, total, qkv, sems
):
    x, shard = where[0], where[1]
    ring = ring_pairs((b0, b1, b2, b3, b4), weight, x)
    made = []
    for yl in range(2):
        pairs = ring[yl::2]
        pairs += [
            (
                normed.at[half * HALF : half * HALF + HALF, yl * 1536 : yl * 1536 + 1536],
                rows.at[yl, half],
            )
            for half in range(2)
        ]
        made.append(start_all(pairs, sems, 7 * yl))
    for yl in range(2):
        for copy in made[yl][:5]:
            copy.wait()
        for half in range(2):
            made[yl][5 + half].wait()
            part = jnp.dot(
                rows[yl, half],
                weight[yl].reshape(1536, 640),
                preferred_element_type=jnp.float32,
            )
            here = slice(half * HALF, half * HALF + HALF)
            if yl == 0:
                total[here] = part
            else:
                qkv[256 + half * HALF : 256 + half * HALF + HALF] = (total[here] + part).astype(
                    jnp.bfloat16
                )
    qkv[0:256] = jnp.zeros((256, 640), jnp.bfloat16)
    row = lax.broadcasted_iota(jnp.int32, (BLK, 3 * BLK), 0)
    column = lax.broadcasted_iota(jnp.int32, (BLK, 3 * BLK), 1)
    causal = (column >= 2 * BLK) & (column - 2 * BLK <= row)
    for block in range(8):
        mine = document_of(lengths, shard, block)
        near, far = (
            (document_of(lengths, shard, block - k) == mine).astype(jnp.int32)
            if block >= k
            else jnp.int32(0)
            for k in (1, 2)
        )
        open_before = jnp.where(column < BLK, far, near)
        allowed = causal | ((column < 2 * BLK) & (open_before == 1))
        at = block * BLK
        window = slice(at, at + 3 * BLK)
        own = slice(at + 2 * BLK, at + 3 * BLK)
        stacked = jnp.concatenate(
            [qkv[own, 256 + i * 128 : 384 + i * 128] for i in range(3)], axis=0
        )
        scores = (
            lax.dot_general(
                stacked,
                qkv[window, 0:128],
                (((1,), (1,)), ((), ())),
                preferred_element_type=jnp.float32,
            )
            * SCALE
        )
        scores = jnp.where(allowed[None], scores.reshape(3, BLK, 3 * BLK), -jnp.inf)
        exponent = jnp.exp(scores - jnp.max(scores, axis=-1, keepdims=True))
        row_total = jnp.sum(exponent, axis=-1, keepdims=True)
        mixed = jnp.dot(
            exponent.astype(jnp.bfloat16).reshape(3 * BLK, 3 * BLK),
            qkv[window, 128:256],
            preferred_element_type=jnp.float32,
        )
        mixed = (mixed / row_total.reshape(3 * BLK, 1)).astype(jnp.bfloat16)
        for i in range(3):
            out[at : at + BLK, i * 128 : i * 128 + 128] = mixed[i * BLK : i * BLK + BLK]


def attend(where, lengths, normed, ring):
    return pl.pallas_call(
        attention_kernel,
        out_shape=jax.ShapeDtypeStruct((2 * HALF, 384), jnp.bfloat16),
        in_specs=[SMEM_SPEC] * 2 + [ANY_SPEC] * 6,
        out_specs=VMEM_SPEC,
        scratch_shapes=[
            pltpu.VMEM((2, 2, HALF, 1536), jnp.bfloat16),
            pltpu.VMEM((2, 8, 4, 48, 640), jnp.bfloat16),
            pltpu.VMEM((2 * HALF, 640), jnp.float32),
            pltpu.VMEM((256 + 2 * HALF, 640), jnp.bfloat16),
            pltpu.SemaphoreType.DMA((14,)),
        ],
        compiler_params=PARAMS,
        name="attend",
    )(where, lengths, normed, *ring)


def output_kernel(
    half, where, lengths, dest, heads, b0, b1, b2, b3, b4, stay, leave, rows, weight, sems
):
    x, shard = where[0], where[1]
    made = start_all(ring_pairs((b0, b1, b2, b3, b4), weight, x), sems, 0)
    parts = start_all(
        [(heads.at[t, pl.ds(half * HALF, HALF)], rows.at[t]) for t in range(8)], sems, 10
    )
    for copy in made:
        copy.wait()
    total = jnp.zeros((HALF, 384), jnp.float32)
    for t in range(8):
        parts[t].wait()
        part = weight[t >> 2, 2 * (t & 3) : 2 * (t & 3) + 2]
        total = total + jnp.dot(
            rows[t], part.reshape(384, 384), preferred_element_type=jnp.float32
        )
    for j in range(4):
        document = document_of(lengths, shard, 4 * half + j)
        target = jnp.where(
            document == 0,
            dest[shard, 0],
            jnp.where(document == 1, dest[shard, 1], dest[shard, 2]),
        )
        moved = (target != shard).astype(jnp.float32)
        here = slice(j * BLK, j * BLK + BLK)
        stay[here] = (total[here] * (1.0 - moved)).astype(jnp.bfloat16)
        leave[here] = (total[here] * moved).astype(jnp.bfloat16)


def project_output(half, where, lengths, dest, heads, ring):
    piece = jax.ShapeDtypeStruct((HALF, 384), jnp.bfloat16)
    return pl.pallas_call(
        functools.partial(output_kernel, half),
        out_shape=(piece, piece),
        in_specs=[SMEM_SPEC] * 3 + [ANY_SPEC] * 6,
        out_specs=(VMEM_SPEC, VMEM_SPEC),
        scratch_shapes=[
            pltpu.VMEM((8, HALF, 384), jnp.bfloat16),
            pltpu.VMEM((2, 8, 4, 48, 384), jnp.bfloat16),
            pltpu.SemaphoreType.DMA((18,)),
        ],
        compiler_params=PARAMS,
        name="project_output",
    )(where, lengths, dest, heads, *ring)


def shards(
    activations,
    norm_gain,
    query_weight,
    key_weight,
    value_matrix,
    output_weight,
    document_lengths,
    doc_dest,
):
    yh = lax.axis_index("yh")
    where = lax.dynamic_index_in_dim(
        jnp.asarray(PLACES), lax.axis_index(AXES), 0, keepdims=False
    )

    inputs = activations.astype(jnp.float32)
    mean_square = jnp.mean(inputs * inputs, axis=1, keepdims=True)
    normed = (inputs * lax.rsqrt(mean_square + EPS) * norm_gain.astype(jnp.float32)).astype(
        jnp.bfloat16
    )
    gathered = lax.all_gather(normed, ("yh", "c"), axis=0, tiled=True)

    packed = jnp.concatenate(
        [
            lax.dynamic_slice_in_dim(key_weight, yh * 128, 128, 1),
            lax.dynamic_slice_in_dim(value_matrix, yh * 128, 128, 1),
            query_weight,
            output_weight,
        ],
        axis=1,
    )
    packed = lax.all_gather(packed, "yl", axis=0, tiled=False)
    ring = ring_x(lax.all_gather(packed[..., 0:640], "z", axis=0, tiled=False))

    attention = attend(where, document_lengths, gathered, ring)
    heads = lax.all_gather(attention, ("yh", "c"), axis=0, tiled=False)

    columns = lax.optimization_barrier((packed[..., 640:1024], attention))[0]
    ring = ring_x(lax.all_gather(columns, "z", axis=0, tiled=False))
    pairs = [(i, (i + 1) % 64) for i in range(64)]
    staying, arrived = [], []
    for half in range(2):
        stay, leave = project_output(half, where, document_lengths, doc_dest, heads, ring)
        staying.append(stay)
        arrived.append(lax.ppermute(leave, ("yl", "z", "x"), pairs))
    return jnp.concatenate(staying + arrived, axis=0)


def solution(mesh):
    fine = Mesh(np.asarray(mesh.devices).reshape(SIZES), AXES)
    dp, tensor = ("yl", "z", "x"), ("yh", "c")
    in_specs = (
        P(dp + tensor, None),
        P(),
        P(dp, tensor),
        P(dp, None),
        P(dp, None),
        P(dp, tensor),
        P(),
        P(),
    )
    return jax.shard_map(
        shards, mesh=fine, in_specs=in_specs, out_specs=P(dp, tensor), check_vma=False
    )
```

```python
import functools
import math

import jax
import jax.numpy as jnp
import numpy as np
from jax import lax
from jax.experimental import pallas as pl
from jax.experimental.pallas import tpu as pltpu
from jax.sharding import Mesh, PartitionSpec as P

BLK = 128
EPS = 1e-05
SCALE = 1.0 / math.sqrt(128)
AXES = ("yl", "z", "x", "yh", "c")
SIZES = (2, 8, 4, 4, 2)
EXTENT = dict(zip(AXES, SIZES))
HALF = 512
PART = 256
VMEM = 56 * 1024 * 1024
PARAMS = pltpu.CompilerParams(vmem_limit_bytes=VMEM)
SMEM_SPEC = pl.BlockSpec(memory_space=pltpu.SMEM)
ANY_SPEC = pl.BlockSpec(memory_space=pl.ANY)
VMEM_SPEC = pl.BlockSpec(memory_space=pltpu.VMEM)
PLACES = np.stack(
    [(np.arange(512) // 8) % 4, np.arange(512) // 8], axis=1
).astype(np.int32)


def shift(value, axis, steps):
    count = EXTENT[axis]
    return lax.ppermute(value, axis, [(i, (i + steps) % count) for i in range(count)])


def ring_x(block):
    half = block.shape[0] // 2
    below = shift(block, "x", 1)
    above = shift(block, "x", -1)
    return (
        block,
        below,
        above,
        shift(below[:half], "x", 1),
        shift(above[half:], "x", -1),
    )


def ring_pairs(refs, weight, x):
    pairs = []
    for ref, first, offset in zip(refs, (0, 0, 0, 0, 4), (0, 3, 1, 2, 2)):
        for yl in range(2):
            pairs.append(
                (ref.at[:, yl], weight.at[yl, pl.ds(first, ref.shape[0]), (x + offset) & 3])
            )
    return pairs


def start_all(pairs, sems, first):
    made = []
    for i, (source, target) in enumerate(pairs):
        copy = pltpu.make_async_copy(source, target, sems.at[first + i])
        copy.start()
        made.append(copy)
    return made


def document_of(lengths, shard, block):
    first_end = lengths[shard, 0]
    second_end = first_end + lengths[shard, 1]
    return (block >= first_end).astype(jnp.int32) + (block >= second_end).astype(jnp.int32)


def attention_kernel(
    where, lengths, normed, b0, b1, b2, b3, b4, out, rows, weight, qkv, sems
):
    x, shard = where[0], where[1]
    made = start_all(ring_pairs((b0, b1, b2, b3, b4), weight, x), sems, 0)

    def start(part):
        return start_all([(normed.at[part * PART : part * PART + PART], rows.at[part])], sems, 10 + part)

    parts = {0: start(0)}
    for copy in made:
        copy.wait()
    parts[1] = start(1)
    qkv[0:256] = jnp.zeros((256, 640), jnp.bfloat16)
    row = lax.broadcasted_iota(jnp.int32, (BLK, 3 * BLK), 0)
    column = lax.broadcasted_iota(jnp.int32, (BLK, 3 * BLK), 1)
    causal = (column >= 2 * BLK) & (column - 2 * BLK <= row)
    for block in range(8):
        if block * BLK % PART == 0:
            part = block * BLK // PART
            parts[part][0].wait()
            if part + 2 < 1024 // PART:
                parts[part + 2] = start(part + 2)
            qkv[256 + part * PART : 256 + part * PART + PART] = jnp.dot(
                rows[part], weight[...].reshape(3072, 640), preferred_element_type=jnp.float32
            ).astype(jnp.bfloat16)
        mine = document_of(lengths, shard, block)
        near, far = (
            (document_of(lengths, shard, block - k) == mine).astype(jnp.int32)
            if block >= k
            else jnp.int32(0)
            for k in (1, 2)
        )
        open_before = jnp.where(column < BLK, far, near)
        allowed = causal | ((column < 2 * BLK) & (open_before == 1))
        at = block * BLK
        window = slice(at, at + 3 * BLK)
        own = slice(at + 2 * BLK, at + 3 * BLK)
        stacked = jnp.concatenate(
            [qkv[own, 256 + i * 128 : 384 + i * 128] for i in range(3)], axis=0
        )
        scores = (
            lax.dot_general(
                stacked,
                qkv[window, 0:128],
                (((1,), (1,)), ((), ())),
                preferred_element_type=jnp.float32,
            )
            * SCALE
        )
        scores = jnp.where(allowed[None], scores.reshape(3, BLK, 3 * BLK), -jnp.inf)
        exponent = jnp.exp(scores - jnp.max(scores, axis=-1, keepdims=True))
        row_total = jnp.sum(exponent, axis=-1, keepdims=True)
        mixed = jnp.dot(
            exponent.astype(jnp.bfloat16).reshape(3 * BLK, 3 * BLK),
            qkv[window, 128:256],
            preferred_element_type=jnp.float32,
        )
        mixed = (mixed / row_total.reshape(3 * BLK, 1)).astype(jnp.bfloat16)
        for i in range(3):
            out[at : at + BLK, i * 128 : i * 128 + 128] = mixed[i * BLK : i * BLK + BLK]


def attend(where, lengths, normed, ring):
    return pl.pallas_call(
        attention_kernel,
        out_shape=jax.ShapeDtypeStruct((2 * HALF, 384), jnp.bfloat16),
        in_specs=[SMEM_SPEC] * 2 + [ANY_SPEC] * 6,
        out_specs=VMEM_SPEC,
        scratch_shapes=[
            pltpu.VMEM((1024 // PART, PART, 3072), jnp.bfloat16),
            pltpu.VMEM((2, 8, 4, 48, 640), jnp.bfloat16),
            pltpu.VMEM((256 + 2 * HALF, 640), jnp.bfloat16),
            pltpu.SemaphoreType.DMA((10 + 1024 // PART,)),
        ],
        compiler_params=PARAMS,
        name="attend",
    )(where, lengths, normed, *ring)


def assemble_kernel(where, b0, b1, b2, b3, b4, out, sems):
    for copy in start_all(ring_pairs((b0, b1, b2, b3, b4), out, where[0]), sems, 0):
        copy.wait()


def assemble(where, ring):
    return pl.pallas_call(
        assemble_kernel,
        out_shape=jax.ShapeDtypeStruct((2, 8, 4, 48, 384), jnp.bfloat16),
        in_specs=[SMEM_SPEC] + [ANY_SPEC] * 5,
        out_specs=VMEM_SPEC,
        scratch_shapes=[pltpu.SemaphoreType.DMA((10,))],
        compiler_params=PARAMS,
        name="assemble",
    )(where, *ring)


def output_kernel(half, where, lengths, dest, heads, weight, *rest):
    result, leave, stay, rows, sems = rest[-5:]
    shard = where[1]
    made = start_all(
        [
            (heads.at[t, half * HALF : half * HALF + HALF], rows.at[:, t * 384 : t * 384 + 384])
            for t in range(8)
        ],
        sems,
        0,
    )
    for copy in made:
        copy.wait()
    total = jnp.dot(
        rows[...], weight[...].reshape(3072, 384), preferred_element_type=jnp.float32
    )
    for j in range(4):
        document = document_of(lengths, shard, 4 * half + j)
        target = jnp.where(
            document == 0,
            dest[shard, 0],
            jnp.where(document == 1, dest[shard, 1], dest[shard, 2]),
        )
        moved = (target != shard).astype(jnp.float32)
        here = slice(j * BLK, j * BLK + BLK)
        stay[here] = (total[here] * (1.0 - moved)).astype(jnp.bfloat16)
        leave[here] = (total[here] * moved).astype(jnp.bfloat16)
    copy = pltpu.make_async_copy(
        stay, result.at[half * HALF : half * HALF + HALF], sems.at[8]
    )
    copy.start()
    copy.wait()


def project_output(half, where, lengths, dest, heads, weight, *result):
    return pl.pallas_call(
        functools.partial(output_kernel, half),
        out_shape=(
            jax.ShapeDtypeStruct((4 * HALF, 384), jnp.bfloat16),
            jax.ShapeDtypeStruct((HALF, 384), jnp.bfloat16),
        ),
        in_specs=[SMEM_SPEC] * 3 + [ANY_SPEC, VMEM_SPEC] + [ANY_SPEC] * len(result),
        out_specs=(ANY_SPEC, VMEM_SPEC),
        scratch_shapes=[
            pltpu.VMEM((HALF, 384), jnp.bfloat16),
            pltpu.VMEM((HALF, 3072), jnp.bfloat16),
            pltpu.SemaphoreType.DMA((9,)),
        ],
        input_output_aliases={5: 0} if result else {},
        cost_estimate=pl.CostEstimate(
            flops=2 * HALF * 3072 * 384, bytes_accessed=6000000, transcendentals=0
        ),
        compiler_params=PARAMS,
        name="project_output",
    )(where, lengths, dest, heads, weight, *result)


def shards(
    activations,
    norm_gain,
    query_weight,
    key_weight,
    value_matrix,
    output_weight,
    document_lengths,
    doc_dest,
):
    yh = lax.axis_index("yh")
    where = lax.dynamic_index_in_dim(
        jnp.asarray(PLACES), lax.axis_index(AXES), 0, keepdims=False
    )

    inputs = activations.astype(jnp.float32)
    mean_square = jnp.mean(inputs * inputs, axis=1, keepdims=True)
    normed = (inputs * lax.rsqrt(mean_square + EPS) * norm_gain.astype(jnp.float32)).astype(
        jnp.bfloat16
    )
    gathered = lax.all_gather(normed, ("yh", "c"), axis=0, tiled=True)

    packed = jnp.concatenate(
        [
            lax.dynamic_slice_in_dim(key_weight, yh * 128, 128, 1),
            lax.dynamic_slice_in_dim(value_matrix, yh * 128, 128, 1),
            query_weight,
            output_weight,
        ],
        axis=1,
    )
    packed = lax.all_gather(packed, "yl", axis=0, tiled=False)
    ring = ring_x(lax.all_gather(packed[..., 0:640], "z", axis=0, tiled=False))

    attention = attend(where, document_lengths, gathered, ring)
    heads = lax.all_gather(attention, ("yh", "c"), axis=0, tiled=False)

    columns = lax.optimization_barrier((packed[..., 640:1024], attention))[0]
    weight = assemble(where, ring_x(lax.all_gather(columns, "z", axis=0, tiled=False)))
    pairs = [(i, (i + 1) % 64) for i in range(64)]
    result, arrived = (), []
    for half in range(2):
        *result, leaving = project_output(
            half, where, document_lengths, doc_dest, heads, weight, *result
        )
        arrived.append(lax.ppermute(leaving, ("yl", "z", "x"), pairs))
    result = result[0]
    for half in range(2):
        result = lax.dynamic_update_slice(result, arrived[half], ((2 + half) * HALF, 0))
    return result


def solution(mesh):
    fine = Mesh(np.asarray(mesh.devices).reshape(SIZES), AXES)
    dp, tensor = ("yl", "z", "x"), ("yh", "c")
    in_specs = (
        P(dp + tensor, None),
        P(),
        P(dp, tensor),
        P(dp, None),
        P(dp, None),
        P(dp, tensor),
        P(),
        P(),
    )
    return jax.shard_map(
        shards, mesh=fine, in_specs=in_specs, out_specs=P(dp, tensor), check_vma=False
    )
```

```python
import functools
import math

import jax
import jax.numpy as jnp
import numpy as np
from jax import lax
from jax.experimental import pallas as pl
from jax.experimental.pallas import tpu as pltpu
from jax.sharding import Mesh, PartitionSpec as P

BLK = 128
EPS = 1e-05
SCALE = 1.0 / math.sqrt(128)
AXES = ("yl", "z", "x", "yh", "c")
SIZES = (2, 8, 4, 4, 2)
EXTENT = dict(zip(AXES, SIZES))
HALF = 512
PART = 256
PARAMS = pltpu.CompilerParams(vmem_limit_bytes=56 * 1024 * 1024)
SMALL_PARAMS = pltpu.CompilerParams(vmem_limit_bytes=46 * 1024 * 1024)
SMEM_SPEC = pl.BlockSpec(memory_space=pltpu.SMEM)
ANY_SPEC = pl.BlockSpec(memory_space=pl.ANY)
HBM_SPEC = pl.BlockSpec(memory_space=pltpu.HBM)
VMEM_SPEC = pl.BlockSpec(memory_space=pltpu.VMEM)
PLACES = np.stack(
    [(np.arange(512) // 8) % 4, np.arange(512) // 8], axis=1
).astype(np.int32)


def shift(value, axis, steps):
    count = EXTENT[axis]
    return lax.ppermute(value, axis, [(i, (i + steps) % count) for i in range(count)])


def ring_x(block):
    half = block.shape[0] // 2
    below = shift(block, "x", 1)
    above = shift(block, "x", -1)
    return (
        block,
        below,
        above,
        shift(below[:half], "x", 1),
        shift(above[half:], "x", -1),
    )


def ring_pairs(refs, weight, x):
    pairs = []
    for ref, first, offset in zip(refs, (0, 0, 0, 0, 4), (0, 3, 1, 2, 2)):
        for yl in range(2):
            pairs.append(
                (ref.at[:, yl], weight.at[yl, pl.ds(first, ref.shape[0]), (x + offset) & 3])
            )
    return pairs


def start_all(pairs, sems, first):
    made = []
    for i, (source, target) in enumerate(pairs):
        copy = pltpu.make_async_copy(source, target, sems.at[first + i])
        copy.start()
        made.append(copy)
    return made


def document_of(lengths, shard, block):
    first_end = lengths[shard, 0]
    second_end = first_end + lengths[shard, 1]
    return (block >= first_end).astype(jnp.int32) + (block >= second_end).astype(jnp.int32)


def attention_kernel(
    where, lengths, normed, b0, b1, b2, b3, b4, out, rows, weight, qkv, sems
):
    x, shard = where[0], where[1]
    made = start_all(ring_pairs((b0, b1, b2, b3, b4), weight, x), sems, 0)

    def start(part):
        return start_all([(normed.at[part * PART : part * PART + PART], rows.at[part])], sems, 10 + part)

    parts = {0: start(0)}
    for copy in made:
        copy.wait()
    parts[1] = start(1)
    qkv[0:256] = jnp.zeros((256, 640), jnp.bfloat16)
    row = lax.broadcasted_iota(jnp.int32, (BLK, 3 * BLK), 0)
    column = lax.broadcasted_iota(jnp.int32, (BLK, 3 * BLK), 1)
    causal = (column >= 2 * BLK) & (column - 2 * BLK <= row)
    for block in range(8):
        if block * BLK % PART == 0:
            part = block * BLK // PART
            parts[part][0].wait()
            if part + 2 < 1024 // PART:
                parts[part + 2] = start(part + 2)
            qkv[256 + part * PART : 256 + part * PART + PART] = jnp.dot(
                rows[part], weight[...].reshape(3072, 640), preferred_element_type=jnp.float32
            ).astype(jnp.bfloat16)
        mine = document_of(lengths, shard, block)
        near, far = (
            (document_of(lengths, shard, block - k) == mine).astype(jnp.int32)
            if block >= k
            else jnp.int32(0)
            for k in (1, 2)
        )
        open_before = jnp.where(column < BLK, far, near)
        allowed = causal | ((column < 2 * BLK) & (open_before == 1))
        at = block * BLK
        window = slice(at, at + 3 * BLK)
        own = slice(at + 2 * BLK, at + 3 * BLK)
        stacked = jnp.concatenate(
            [qkv[own, 256 + i * 128 : 384 + i * 128] for i in range(3)], axis=0
        )
        scores = (
            lax.dot_general(
                stacked,
                qkv[window, 0:128],
                (((1,), (1,)), ((), ())),
                preferred_element_type=jnp.float32,
            )
            * SCALE
        )
        scores = jnp.where(allowed[None], scores.reshape(3, BLK, 3 * BLK), -jnp.inf)
        exponent = jnp.exp(scores - jnp.max(scores, axis=-1, keepdims=True))
        row_total = jnp.sum(exponent, axis=-1, keepdims=True)
        mixed = jnp.dot(
            exponent.astype(jnp.bfloat16).reshape(3 * BLK, 3 * BLK),
            qkv[window, 128:256],
            preferred_element_type=jnp.float32,
        )
        mixed = (mixed / row_total.reshape(3 * BLK, 1)).astype(jnp.bfloat16)
        for i in range(3):
            out[at : at + BLK, i * 128 : i * 128 + 128] = mixed[i * BLK : i * BLK + BLK]


def attend(where, lengths, normed, ring):
    return pl.pallas_call(
        attention_kernel,
        out_shape=jax.ShapeDtypeStruct((2 * HALF, 384), jnp.bfloat16),
        in_specs=[SMEM_SPEC] * 2 + [HBM_SPEC] + [ANY_SPEC] * 5,
        out_specs=VMEM_SPEC,
        scratch_shapes=[
            pltpu.VMEM((1024 // PART, PART, 3072), jnp.bfloat16),
            pltpu.VMEM((2, 8, 4, 48, 640), jnp.bfloat16),
            pltpu.VMEM((256 + 2 * HALF, 640), jnp.bfloat16),
            pltpu.SemaphoreType.DMA((10 + 1024 // PART,)),
        ],
        compiler_params=PARAMS,
        name="attend",
    )(where, lengths, normed, *ring)


def assemble_kernel(where, b0, b1, b2, b3, b4, out, sems):
    for copy in start_all(ring_pairs((b0, b1, b2, b3, b4), out, where[0]), sems, 0):
        copy.wait()


def assemble(where, ring):
    return pl.pallas_call(
        assemble_kernel,
        out_shape=jax.ShapeDtypeStruct((2, 8, 4, 48, 384), jnp.bfloat16),
        in_specs=[SMEM_SPEC] + [ANY_SPEC] * 5,
        out_specs=VMEM_SPEC,
        scratch_shapes=[pltpu.SemaphoreType.DMA((10,))],
        compiler_params=SMALL_PARAMS,
        name="assemble",
    )(where, *ring)


def output_kernel(half, where, lengths, dest, heads, weight, *rest):
    result, leave, stay, rows, sems = rest[-5:]
    shard = where[1]
    made = start_all(
        [
            (heads.at[t, half * HALF : half * HALF + HALF], rows.at[:, t * 384 : t * 384 + 384])
            for t in range(8)
        ],
        sems,
        0,
    )
    total = jnp.zeros((HALF, 384), jnp.float32)
    for yl in range(2):
        for copy in made[4 * yl : 4 * yl + 4]:
            copy.wait()
        total = total + jnp.dot(
            rows[:, yl * 1536 : yl * 1536 + 1536],
            weight[yl].reshape(1536, 384),
            preferred_element_type=jnp.float32,
        )
    moved = []
    for j in range(4):
        document = document_of(lengths, shard, 4 * half + j)
        target = jnp.where(
            document == 0,
            dest[shard, 0],
            jnp.where(document == 1, dest[shard, 1], dest[shard, 2]),
        )
        moved.append((target != shard).astype(jnp.float32))
        here = slice(j * BLK, j * BLK + BLK)
        stay[here] = (total[here] * (1.0 - moved[j])).astype(jnp.bfloat16)
    copy = pltpu.make_async_copy(
        stay, result.at[half * HALF : half * HALF + HALF], sems.at[8]
    )
    copy.start()
    for j in range(4):
        here = slice(j * BLK, j * BLK + BLK)
        leave[here] = (total[here] * moved[j]).astype(jnp.bfloat16)
    copy.wait()


def project_output(half, where, lengths, dest, heads, weight, *result):
    return pl.pallas_call(
        functools.partial(output_kernel, half),
        out_shape=(
            jax.ShapeDtypeStruct((4 * HALF, 384), jnp.bfloat16),
            jax.ShapeDtypeStruct((HALF, 384), jnp.bfloat16),
        ),
        in_specs=[SMEM_SPEC] * 3 + [HBM_SPEC, VMEM_SPEC] + [HBM_SPEC] * len(result),
        out_specs=(HBM_SPEC, VMEM_SPEC),
        scratch_shapes=[
            pltpu.VMEM((HALF, 384), jnp.bfloat16),
            pltpu.VMEM((HALF, 3072), jnp.bfloat16),
            pltpu.SemaphoreType.DMA((9,)),
        ],
        input_output_aliases={5: 0} if result else {},
        cost_estimate=pl.CostEstimate(
            flops=2 * HALF * 3072 * 384, bytes_accessed=6000000, transcendentals=0
        ),
        compiler_params=SMALL_PARAMS,
        name="project_output",
    )(where, lengths, dest, heads, weight, *result)


def shards(
    activations,
    norm_gain,
    query_weight,
    key_weight,
    value_matrix,
    output_weight,
    document_lengths,
    doc_dest,
):
    yh = lax.axis_index("yh")
    where = lax.dynamic_index_in_dim(
        jnp.asarray(PLACES), lax.axis_index(AXES), 0, keepdims=False
    )

    inputs = activations.astype(jnp.float32)
    mean_square = jnp.mean(inputs * inputs, axis=1, keepdims=True)
    normed = (inputs * lax.rsqrt(mean_square + EPS) * norm_gain.astype(jnp.float32)).astype(
        jnp.bfloat16
    )
    gathered = lax.all_gather(normed, ("yh", "c"), axis=0, tiled=True)

    packed = jnp.concatenate(
        [
            lax.dynamic_slice_in_dim(key_weight, yh * 128, 128, 1),
            lax.dynamic_slice_in_dim(value_matrix, yh * 128, 128, 1),
            query_weight,
            output_weight,
        ],
        axis=1,
    )
    packed = lax.all_gather(packed, "yl", axis=0, tiled=False)
    ring = ring_x(lax.all_gather(packed[..., 0:640], "z", axis=0, tiled=False))

    attention = attend(where, document_lengths, gathered, ring)
    heads = lax.all_gather(attention, ("yh", "c"), axis=0, tiled=False)

    columns = lax.optimization_barrier((packed[..., 640:1024], attention))[0]
    weight = assemble(where, ring_x(lax.all_gather(columns, "z", axis=0, tiled=False)))
    pairs = [(i, (i + 1) % 64) for i in range(64)]
    result, arrived = (), []
    for half in range(2):
        *result, leaving = project_output(
            half, where, document_lengths, doc_dest, heads, weight, *result
        )
        arrived.append(lax.ppermute(leaving, ("yl", "z", "x"), pairs))
    result = result[0]
    for half in range(2):
        result = lax.dynamic_update_slice(result, arrived[half], ((2 + half) * HALF, 0))
    return result


def solution(mesh):
    fine = Mesh(np.asarray(mesh.devices).reshape(SIZES), AXES)
    dp, tensor = ("yl", "z", "x"), ("yh", "c")
    in_specs = (
        P(dp + tensor, None),
        P(),
        P(dp, tensor),
        P(dp, None),
        P(dp, None),
        P(dp, tensor),
        P(),
        P(),
    )
    return jax.shard_map(
        shards, mesh=fine, in_specs=in_specs, out_specs=P(dp, tensor), check_vma=False
    )
```

```python
import functools
import math

import jax
import jax.numpy as jnp
import numpy as np
from jax import lax
from jax.experimental import pallas as pl
from jax.experimental.pallas import tpu as pltpu
from jax.sharding import Mesh, PartitionSpec as P

BLK = 128
EPS = 1e-05
SCALE = 1.0 / math.sqrt(128)
AXES = ("yl", "z", "x", "yh", "c")
SIZES = (2, 8, 4, 4, 2)
EXTENT = dict(zip(AXES, SIZES))
HALF = 512
PART = 256
PARAMS = pltpu.CompilerParams(vmem_limit_bytes=56 * 1024 * 1024)
SMALL_PARAMS = pltpu.CompilerParams(vmem_limit_bytes=46 * 1024 * 1024)
SMEM_SPEC = pl.BlockSpec(memory_space=pltpu.SMEM)
ANY_SPEC = pl.BlockSpec(memory_space=pl.ANY)
HBM_SPEC = pl.BlockSpec(memory_space=pltpu.HBM)
VMEM_SPEC = pl.BlockSpec(memory_space=pltpu.VMEM)
PLACES = np.stack(
    [(np.arange(512) // 8) % 4, np.arange(512) // 8], axis=1
).astype(np.int32)


def shift(value, axis, steps):
    count = EXTENT[axis]
    return lax.ppermute(value, axis, [(i, (i + steps) % count) for i in range(count)])


def ring_x(block):
    half = block.shape[0] // 2
    below = shift(block, "x", 1)
    above = shift(block, "x", -1)
    return (
        block,
        below,
        above,
        shift(below[:half], "x", 1),
        shift(above[half:], "x", -1),
    )


def ring_pairs(refs, weight, x):
    pairs = []
    for ref, first, offset in zip(refs, (0, 0, 0, 0, 4), (0, 3, 1, 2, 2)):
        for yl in range(2):
            pairs.append(
                (ref.at[:, yl], weight.at[yl, pl.ds(first, ref.shape[0]), (x + offset) & 3])
            )
    return pairs


def start_all(pairs, sems, first):
    made = []
    for i, (source, target) in enumerate(pairs):
        copy = pltpu.make_async_copy(source, target, sems.at[first + i])
        copy.start()
        made.append(copy)
    return made


def document_of(lengths, shard, block):
    first_end = lengths[shard, 0]
    second_end = first_end + lengths[shard, 1]
    return (block >= first_end).astype(jnp.int32) + (block >= second_end).astype(jnp.int32)


def attention_kernel(
    where, lengths, normed, b0, b1, b2, b3, b4, out, rows, weight, qkv, sems
):
    x, shard = where[0], where[1]
    made = start_all(ring_pairs((b0, b1, b2, b3, b4), weight, x), sems, 0)

    def start(part):
        return start_all([(normed.at[part * PART : part * PART + PART], rows.at[part])], sems, 10 + part)

    parts = {0: start(0)}
    for copy in made:
        copy.wait()
    parts[1] = start(1)
    qkv[0:256] = jnp.zeros((256, 640), jnp.bfloat16)
    row = lax.broadcasted_iota(jnp.int32, (BLK, 3 * BLK), 0)
    column = lax.broadcasted_iota(jnp.int32, (BLK, 3 * BLK), 1)
    causal = (column >= 2 * BLK) & (column - 2 * BLK <= row)
    for block in range(8):
        if block * BLK % PART == 0:
            part = block * BLK // PART
            parts[part][0].wait()
            if part + 2 < 1024 // PART:
                parts[part + 2] = start(part + 2)
            qkv[256 + part * PART : 256 + part * PART + PART] = jnp.dot(
                rows[part], weight[...].reshape(3072, 640), preferred_element_type=jnp.float32
            ).astype(jnp.bfloat16)
        mine = document_of(lengths, shard, block)
        near, far = (
            (document_of(lengths, shard, block - k) == mine).astype(jnp.int32)
            if block >= k
            else jnp.int32(0)
            for k in (1, 2)
        )
        open_before = jnp.where(column < BLK, far, near)
        allowed = causal | ((column < 2 * BLK) & (open_before == 1))
        at = block * BLK
        window = slice(at, at + 3 * BLK)
        own = slice(at + 2 * BLK, at + 3 * BLK)
        stacked = jnp.concatenate(
            [qkv[own, 256 + i * 128 : 384 + i * 128] for i in range(3)], axis=0
        )
        scores = (
            lax.dot_general(
                stacked,
                qkv[window, 0:128],
                (((1,), (1,)), ((), ())),
                preferred_element_type=jnp.float32,
            )
            * SCALE
        )
        scores = jnp.where(allowed[None], scores.reshape(3, BLK, 3 * BLK), -jnp.inf)
        exponent = jnp.exp(scores - jnp.max(scores, axis=-1, keepdims=True))
        row_total = jnp.sum(exponent, axis=-1, keepdims=True)
        mixed = jnp.dot(
            exponent.astype(jnp.bfloat16).reshape(3 * BLK, 3 * BLK),
            qkv[window, 128:256],
            preferred_element_type=jnp.float32,
        )
        mixed = (mixed / row_total.reshape(3 * BLK, 1)).astype(jnp.bfloat16)
        for i in range(3):
            out[at : at + BLK, i * 128 : i * 128 + 128] = mixed[i * BLK : i * BLK + BLK]


def attend(where, lengths, normed, ring):
    return pl.pallas_call(
        attention_kernel,
        out_shape=jax.ShapeDtypeStruct((2 * HALF, 384), jnp.bfloat16),
        in_specs=[SMEM_SPEC] * 2 + [HBM_SPEC] + [ANY_SPEC] * 5,
        out_specs=VMEM_SPEC,
        scratch_shapes=[
            pltpu.VMEM((1024 // PART, PART, 3072), jnp.bfloat16),
            pltpu.VMEM((2, 8, 4, 48, 640), jnp.bfloat16),
            pltpu.VMEM((256 + 2 * HALF, 640), jnp.bfloat16),
            pltpu.SemaphoreType.DMA((10 + 1024 // PART,)),
        ],
        compiler_params=PARAMS,
        name="attend",
    )(where, lengths, normed, *ring)


def assemble_kernel(where, b0, b1, b2, b3, b4, out, sems):
    for copy in start_all(ring_pairs((b0, b1, b2, b3, b4), out, where[0]), sems, 0):
        copy.wait()


def assemble(where, ring):
    return pl.pallas_call(
        assemble_kernel,
        out_shape=jax.ShapeDtypeStruct((2, 8, 4, 48, 384), jnp.bfloat16),
        in_specs=[SMEM_SPEC] + [ANY_SPEC] * 5,
        out_specs=VMEM_SPEC,
        scratch_shapes=[pltpu.SemaphoreType.DMA((10,))],
        compiler_params=SMALL_PARAMS,
        name="assemble",
    )(where, *ring)


def output_kernel(half, where, lengths, dest, heads, weight, *rest):
    result, leave, stay, rows, sems = rest[-5:]
    shard = where[1]
    made = start_all(
        [
            (heads.at[t, half * HALF : half * HALF + HALF], rows.at[:, t * 384 : t * 384 + 384])
            for t in range(8)
        ],
        sems,
        0,
    )
    total = jnp.zeros((HALF, 384), jnp.float32)
    for yl in range(2):
        for copy in made[4 * yl : 4 * yl + 4]:
            copy.wait()
        total = total + jnp.dot(
            rows[:, yl * 1536 : yl * 1536 + 1536],
            weight[yl].reshape(1536, 384),
            preferred_element_type=jnp.float32,
        )
    moved = []
    for j in range(4):
        document = document_of(lengths, shard, 4 * half + j)
        target = jnp.where(
            document == 0,
            dest[shard, 0],
            jnp.where(document == 1, dest[shard, 1], dest[shard, 2]),
        )
        moved.append((target != shard).astype(jnp.float32))
        here = slice(j * BLK, j * BLK + BLK)
        stay[here] = (total[here] * (1.0 - moved[j])).astype(jnp.bfloat16)
    copy = pltpu.make_async_copy(
        stay, result.at[half * HALF : half * HALF + HALF], sems.at[8]
    )
    copy.start()
    for j in range(4):
        here = slice(j * BLK, j * BLK + BLK)
        leave[here] = (total[here] * moved[j]).astype(jnp.bfloat16)
    copy.wait()


def project_output(half, where, lengths, dest, heads, weight, *result):
    return pl.pallas_call(
        functools.partial(output_kernel, half),
        out_shape=(
            jax.ShapeDtypeStruct((4 * HALF, 384), jnp.bfloat16),
            jax.ShapeDtypeStruct((HALF, 384), jnp.bfloat16),
        ),
        in_specs=[SMEM_SPEC] * 3 + [HBM_SPEC, VMEM_SPEC] + [HBM_SPEC] * len(result),
        out_specs=(HBM_SPEC, VMEM_SPEC),
        scratch_shapes=[
            pltpu.VMEM((HALF, 384), jnp.bfloat16),
            pltpu.VMEM((HALF, 3072), jnp.bfloat16),
            pltpu.SemaphoreType.DMA((9,)),
        ],
        input_output_aliases={5: 0} if result else {},
        cost_estimate=pl.CostEstimate(
            flops=2 * HALF * 3072 * 384, bytes_accessed=6000000, transcendentals=0
        ),
        compiler_params=SMALL_PARAMS,
        name="project_output",
    )(where, lengths, dest, heads, weight, *result)


def norm_kernel(inputs, gain, out):
    values = inputs[...].astype(jnp.float32)
    mean_square = jnp.mean(values * values, axis=1, keepdims=True)
    out[...] = (
        values * lax.rsqrt(mean_square + EPS) * gain[...].astype(jnp.float32)
    ).astype(jnp.bfloat16)


def normalize(activations, gain):
    return pl.pallas_call(
        norm_kernel,
        out_shape=jax.ShapeDtypeStruct(activations.shape, jnp.bfloat16),
        in_specs=[VMEM_SPEC] * 2,
        out_specs=VMEM_SPEC,
        compiler_params=SMALL_PARAMS,
        name="normalize",
    )(activations, gain.reshape(1, -1))


def shards(
    activations,
    norm_gain,
    query_weight,
    key_weight,
    value_matrix,
    output_weight,
    document_lengths,
    doc_dest,
):
    yh = lax.axis_index("yh")
    where = lax.dynamic_index_in_dim(
        jnp.asarray(PLACES), lax.axis_index(AXES), 0, keepdims=False
    )

    normed = normalize(activations, norm_gain)
    gathered = lax.all_gather(normed, ("yh", "c"), axis=0, tiled=True)

    packed = jnp.concatenate(
        [
            lax.dynamic_slice_in_dim(key_weight, yh * 128, 128, 1),
            lax.dynamic_slice_in_dim(value_matrix, yh * 128, 128, 1),
            query_weight,
            output_weight,
        ],
        axis=1,
    )
    packed = lax.all_gather(packed, "yl", axis=0, tiled=False)
    ring = ring_x(lax.all_gather(packed[..., 0:640], "z", axis=0, tiled=False))

    attention = attend(where, document_lengths, gathered, ring)
    heads = lax.all_gather(attention, ("yh", "c"), axis=0, tiled=False)

    columns = lax.optimization_barrier((packed[..., 640:1024], attention))[0]
    weight = assemble(where, ring_x(lax.all_gather(columns, "z", axis=0, tiled=False)))
    pairs = [(i, (i + 1) % 64) for i in range(64)]
    result, arrived = (), []
    for half in range(2):
        *result, leaving = project_output(
            half, where, document_lengths, doc_dest, heads, weight, *result
        )
        arrived.append(lax.ppermute(leaving, ("yl", "z", "x"), pairs))
    result = result[0]
    for half in range(2):
        result = lax.dynamic_update_slice(result, arrived[half], ((2 + half) * HALF, 0))
    return result


def solution(mesh):
    fine = Mesh(np.asarray(mesh.devices).reshape(SIZES), AXES)
    dp, tensor = ("yl", "z", "x"), ("yh", "c")
    in_specs = (
        P(dp + tensor, None),
        P(),
        P(dp, tensor),
        P(dp, None),
        P(dp, None),
        P(dp, tensor),
        P(),
        P(),
    )
    return jax.shard_map(
        shards, mesh=fine, in_specs=in_specs, out_specs=P(dp, tensor), check_vma=False
    )
```
